1024 devices in a mesh: replica: 4 (over y_lo, core), fsdp: 256 (over z, y_hi, x).
Axes of the slice: x: 4, y: 4 (y_hi: 2, y_lo: 2; y = y_hi * 2 + y_lo), z: 32, core: 2. Of those that a mesh axis runs over, the one named last changes fastest.
Arguments:
- inner_stack: bfloat16 [4, 4, 4096, 512], P('replica', None, 'fsdp'), may hold values from -6 to 6
- outer_stack: float32 [4, 4096, 512], P(None, 'fsdp'), may hold values from -6 to 6
- outer_moment: float32 [4, 4096, 512], P(None, 'fsdp'), may hold values from -4 to 4
- layer_ids: int32 [4], replicated, may hold values from 0 to 3, each once
- step_count: int32 [1], replicated, may hold values from 0 to 63
- activations: bfloat16 [262144, 4096], P(('replica', 'fsdp')), may hold values from -24 to 24
- cotangent: bfloat16 [262144, 512], P(('replica', 'fsdp')), may hold values from -0.0625 to 0.0625
- key_weight: bfloat16 [4, 4096, 512], P('replica', 'fsdp'), may hold values from -6 to 6
- first_moment: float32 [4, 4096, 512], P('replica', 'fsdp'), may hold values from -4 to 4
- second_moment: float32 [4, 4096, 512], P('replica', 'fsdp'), may hold values from 0.05 to 2
Outputs:
- inner_out: bfloat16 [4, 4, 4096, 512], P('replica', None, 'fsdp')
- outer_out: float32 [4, 4096, 512], P(None, 'fsdp')
- moment_out: float32 [4, 4096, 512], P(None, 'fsdp')
- key_out: bfloat16 [4, 4096, 512], P('replica', 'fsdp')
- first_out: float32 [4, 4096, 512], P('replica', 'fsdp')
- second_out: float32 [4, 4096, 512], P('replica', 'fsdp')
The draws below stay inside these ranges and needn't reach their ends.
Inputs may be any that keep to these rules, and one draw needn't show every extreme that they name: `layer_ids`: each layer index appears once.
All inputs are finite; a program needn't handle non-finite values.
Results may differ from the reference program's by a relative error of at most 0.012.
Values may be sent and summed in bfloat16 or wider, within the bound.
A program may use at most 32 MiB of HBM per device.

```python
import math
import jax
import jax.numpy as jnp
from jax import lax

DIN = 4096
DKV = 512
BLOCK = 128
LAYERS = 4
FRAG_LAYERS = 1
FRAGS = 4
TOK_DEV = 256
REPLICAS = 4
GROUP_TOK = 65536
TOKENS = 262144
N_FSDP = 256


def with_spikes(values, rng, source, target, shards_of, factor):
    def block_of(dim):
        return (jnp.arange(values.shape[dim]) // (values.shape[dim] // shards_of)).reshape((-1,) + (1,) * (values.ndim - 1 - dim))

    first = jax.random.permutation(rng, shards_of)[block_of(target)]
    far = (block_of(target) + shards_of // 2) % shards_of
    return jnp.where((block_of(source) == first) | (block_of(source) == far), factor * values, values)


def level_of(rng, dims, cuts, smallest, top_value):
    def one(axis_at, shards_of):
        steps = jax.random.uniform(jax.random.fold_in(jax.random.fold_in(rng, 6), axis_at), (shards_of,), jnp.float32, smallest / len(cuts), top_value / len(cuts))
        return jnp.repeat(jnp.exp(steps), dims[axis_at] // shards_of).reshape((-1,) + (1,) * (len(dims) - axis_at - 1))

    factor_of = one(*cuts[0])
    for cut in cuts[1:]:
        factor_of = factor_of * one(*cut)
    return factor_of


def bell_draw(own_key, extent, width, most, cuts=(), dtype=jnp.bfloat16):
    gain = level_of(own_key, extent, cuts, -0.22, 0.18) if cuts else 1.0
    values = jax.random.normal(own_key, extent, jnp.float32) * width * gain
    return jnp.minimum(jnp.maximum(values, -most), most).astype(dtype)


def heavy_noise(rng, extent, width, limit, cuts, heavy, kind=jnp.bfloat16):
    values = width * jax.random.normal(rng, extent, jnp.float32)
    if cuts:
        values = values * level_of(rng, extent, cuts, -0.22, 0.18)
    return jnp.clip(with_spikes(values, jax.random.fold_in(rng, 3), *heavy), -limit, limit).astype(kind)


def setup_inputs(seed: int = 0) -> dict:
    keys = jax.random.split(jax.random.key(seed), 11)
    return {
        "inner_stack": bell_draw(keys[0], (REPLICAS, LAYERS, DIN, DKV), 1.0, 6.0, ((0, 4), (2, 256))),
        "outer_stack": bell_draw(keys[1], (LAYERS, DIN, DKV), 1.0, 6.0, ((1, 256),), jnp.float32),
        "outer_moment": bell_draw(keys[2], (LAYERS, DIN, DKV), 0.3, 4.0, ((1, 256),), jnp.float32),
        "layer_ids": jax.random.permutation(keys[3], LAYERS).astype(jnp.int32),
        "step_count": jax.random.randint(keys[4], (1,), 0, 64).astype(jnp.int32),
        "activations": heavy_noise(keys[5], (TOKENS, DIN), 1.0, 24.0, ((0, 1024),), (0, 1, 1024, 6.0)),
        "cotangent": bell_draw(keys[6], (TOKENS, DKV), (GROUP_TOK ** -0.5), 0.0625, ((0, 1024),)),
        "key_weight": bell_draw(keys[7], (REPLICAS, DIN, DKV), 0.5, 6.0, ((0, 4), (1, 256))),
        "first_moment": bell_draw(keys[8], (REPLICAS, DIN, DKV), 0.3, 4.0, ((0, 4), (1, 256)), jnp.float32),
        "second_moment": jnp.clip(jnp.exp(math.log(2.0) - 3.6888794 * jax.random.uniform(keys[9], (REPLICAS, DIN, DKV), jnp.float32) ** level_of(keys[9], (REPLICAS, DIN, DKV), ((0, 4), (1, 256)), -0.2, 0.2)), 0.05, 2.0),
    }


BETA_FIRST = 0.9
BETA_SECOND = 0.95
INNER_RATE = 0.05
DECAY_RATE = 0.1
ADAM_EPSILON = 1e-08
OUTER_RATE = 0.7
OUTER_MOMENTUM = 0.9
CODE_LIMIT = 448.0
SCALE_EPSILON = 1e-06

def fragment_ids(layer_ids, step_count):
    fragment = (step_count[0] % FRAGS).astype(jnp.int32)
    return lax.dynamic_slice(layer_ids, (fragment * FRAG_LAYERS,), (FRAG_LAYERS,))

def encode_blocks(deltas):
    shaped = deltas.reshape(deltas.shape[:-1] + (deltas.shape[-1] // BLOCK, BLOCK))
    scales = lax.optimization_barrier(jnp.max(jnp.abs(shaped), axis=-1)) / CODE_LIMIT + SCALE_EPSILON
    encoded = (shaped / scales[..., None]).astype(jnp.bfloat16)
    return (encoded, scales)

def decode_blocks(encoded, scales):
    decoded = encoded.astype(jnp.float32) * scales[..., None]
    return decoded.reshape(decoded.shape[:-2] + (decoded.shape[-2] * decoded.shape[-1],))

def outer_update(outer_frag, moment_frag, summed, groups):
    average = summed / groups
    moment_new = OUTER_MOMENTUM * moment_frag + average
    outer_new = outer_frag - OUTER_RATE * (OUTER_MOMENTUM * moment_new + average)
    return (outer_new, moment_new)

def adam_update(weight, first, second, gradient, step_count):
    counter = (step_count[0] + 1).astype(jnp.float32)
    first_new = BETA_FIRST * first + (1.0 - BETA_FIRST) * gradient
    second_new = BETA_SECOND * second + (1.0 - BETA_SECOND) * gradient * gradient
    first_hat = first_new / (1.0 - jnp.power(jnp.float32(BETA_FIRST), counter))
    second_hat = second_new / (1.0 - jnp.power(jnp.float32(BETA_SECOND), counter))
    widened = weight.astype(jnp.float32)
    moved = widened - INNER_RATE * (first_hat / (jnp.sqrt(second_hat) + ADAM_EPSILON) + DECAY_RATE * widened)
    return (moved.astype(jnp.bfloat16), first_new, second_new)

def reference(inner_stack, outer_stack, outer_moment, layer_ids, step_count, activations, cotangent, key_weight, first_moment, second_moment):
    frag_ids = fragment_ids(layer_ids, step_count)
    outer_frag = jnp.take(outer_stack, frag_ids, axis=0)
    moment_frag = jnp.take(outer_moment, frag_ids, axis=0)
    inner_frag = jnp.take(inner_stack, frag_ids, axis=1).astype(jnp.float32)
    deltas = outer_frag[None] - inner_frag
    encoded, scales = encode_blocks(deltas)
    summed = lax.optimization_barrier(jnp.sum(decode_blocks(encoded, scales), axis=0))
    outer_new, moment_new = outer_update(outer_frag, moment_frag, summed, REPLICAS)
    outer_out = outer_stack.at[frag_ids].set(outer_new)
    moment_out = outer_moment.at[frag_ids].set(moment_new)
    rounded = jnp.broadcast_to(outer_new.astype(jnp.bfloat16)[None], inner_frag.shape)
    inner_out = inner_stack.at[:, frag_ids].set(rounded)
    shards = activations.reshape(REPLICAS, N_FSDP, TOK_DEV, DIN)
    cotangents = cotangent.reshape(REPLICAS, N_FSDP, TOK_DEV, DKV)

    def replica_grad(operands):

        def add_term(running, pieces):
            partial_term = lax.dot_general(pieces[0], pieces[1], (((0,), (0,)), ((), ())), preferred_element_type=jnp.float32)
            return (running + partial_term, None)
        initial = jnp.zeros((DIN, DKV), jnp.float32)
        result, unused = lax.scan(add_term, initial, operands)
        return result
    gradient = lax.map(replica_grad, (shards, cotangents))
    key_out, first_out, second_out = adam_update(key_weight, first_moment, second_moment, gradient, step_count)
    return (inner_out, outer_out, moment_out, key_out, first_out, second_out)
```

```python
import jax
import jax.numpy as jnp
from jax import lax
from jax.experimental import pallas as pl
from jax.experimental.pallas import tpu as pltpu
from jax.sharding import PartitionSpec as P

BLOCK = 128
FRAG_LAYERS = 1
FRAGS = 4

BETA_FIRST = 0.9
BETA_SECOND = 0.95
INNER_RATE = 0.05
DECAY_RATE = 0.1
ADAM_EPSILON = 1e-08
OUTER_RATE = 0.7
OUTER_MOMENTUM = 0.9
CODE_LIMIT = 448.0
SCALE_EPSILON = 1e-06

ROWS = 16
COLS = 512
PLANES = 8
BLOCKS = 32
MESH = pl.DeviceIdType.MESH

CHUNKS = (
    (4, "aby"),
    (3, "bay"),
    (5, "yab"),
    (2, "aby"),
    (6, "bay"),
    (1, "yba"),
    (7, "aby"),
    (0, "bay"),
)
LAGS = (2, 3, 4, 5)


def outer_update(outer_frag, moment_frag, summed, groups):
    average = summed / groups
    moment_new = OUTER_MOMENTUM * moment_frag + average
    outer_new = outer_frag - OUTER_RATE * (OUTER_MOMENTUM * moment_new + average)
    return (outer_new, moment_new)


def adam_update(weight, first, second, gradient, step_count):
    counter = (step_count[0] + 1).astype(jnp.float32)
    first_new = BETA_FIRST * first + (1.0 - BETA_FIRST) * gradient
    second_new = BETA_SECOND * second + (1.0 - BETA_SECOND) * gradient * gradient
    first_hat = first_new / (1.0 - jnp.power(jnp.float32(BETA_FIRST), counter))
    second_hat = second_new / (1.0 - jnp.power(jnp.float32(BETA_SECOND), counter))
    widened = weight.astype(jnp.float32)
    moved = widened - INNER_RATE * (
        first_hat / (jnp.sqrt(second_hat) + ADAM_EPSILON) + DECAY_RATE * widened
    )
    return (moved.astype(jnp.bfloat16), first_new, second_new)


def exchange(
    step_ref, ids_ref, inner_ref, outer_ref, act_ref, cot_ref,
    grad_ref, sum_ref,
    work, got0, got1, got2, got3, got4, terms,
    send, recv, term_send, term_recv,
):
    rep = lax.axis_index("replica")
    me = lax.axis_index("fsdp")
    x = lax.rem(me, 4)
    y = lax.rem(me // 4, 2)
    z = me // 8
    low = lax.rem(z, 4)
    high = z // 4
    a = lax.rem((x + 1) // 2, 2)
    b = x // 2

    def at(x_to, y_to, low_to, high_to):
        return (rep, ((high_to * 4 + low_to) * 2 + y_to) * 4 + x_to)

    near = {
        "a": at(x + 1 - 2 * lax.rem(x, 2), y, low, high),
        "b": at(3 - x, y, low, high),
        "y": at(x, 1 - y, low, high),
    }
    lows = [at(x, y, lax.rem(low + i, 4), high) for i in range(1, 4)]
    highs = {d: at(x, y, low, lax.rem(high + d, PLANES)) for d in range(1, PLANES)}
    reps = [(lax.rem(rep + i, 4), me) for i in range(1, 4)]

    barrier = pltpu.get_barrier_semaphore()
    peers = [*near.values(), *lows, *highs.values(), *reps]
    for peer in peers:
        pl.semaphore_signal(barrier, inc=1, device_id=peer, device_id_type=MESH)

    def remote(src, dst, sems, k, peer):
        return pltpu.make_async_remote_copy(
            src_ref=src, dst_ref=dst, send_sem=sems[0].at[k], recv_sem=sems[1].at[k],
            device_id=peer, device_id_type=MESH,
        )

    frag = ids_ref[lax.rem(step_ref[0], FRAGS)]
    deltas = outer_ref[frag] - inner_ref[0, frag].astype(jnp.float32)
    for k in range(COLS // BLOCK):
        part = deltas[:, k * BLOCK : (k + 1) * BLOCK]
        scale = jnp.max(jnp.abs(part), axis=-1, keepdims=True) / CODE_LIMIT + SCALE_EPSILON
        coded = (part / scale).astype(jnp.bfloat16).astype(jnp.float32)
        terms[rep, :, k * BLOCK : (k + 1) * BLOCK] = (coded * scale).astype(jnp.bfloat16)

    def multiply(c):
        ahead, order = CHUNKS[c]
        first = pl.multiple_of(lax.rem(high + ahead, PLANES) * 512, 512)
        part = lax.dot_general(
            act_ref[:, pl.ds(first, 512)], cot_ref[...], (((0,), (0,)), ((), ())),
            preferred_element_type=jnp.float32,
        ).astype(jnp.bfloat16)
        for n in range(BLOCKS):
            low_to, y_to, x_to = n // 8, (n // 4) % 2, n % 4
            off = {
                "a": lax.rem(a + ((x_to + 1) // 2) % 2, 2),
                "b": lax.rem(b + x_to // 2, 2),
                "y": lax.rem(y + y_to, 2),
            }
            place = lax.rem(low_to - low + 4, 4)
            for weight, axis in zip((16, 8, 4), order):
                place = place + off[axis] * weight
            work[c, place] = part[n * ROWS : (n + 1) * ROWS]

    def sends(c, stage):
        ahead, order = CHUNKS[c]
        sems = (send.at[c], recv.at[c])
        if stage < 3:
            got, n = ((got0, 16), (got1, 8), (got2, 4))[stage]
            return [remote(work.at[c, pl.ds(n, n)], got.at[c], sems, stage, near[order[stage]])]
        if stage == 3:
            return [
                remote(work.at[c, i], got3.at[c, i - 1], sems, 2 + i, lows[i - 1])
                for i in range(1, 4)
            ]
        return [remote(work.at[c, 0], got4.at[ahead - 1], sems, 6, highs[ahead])] if ahead else []

    def add(c, got, n):
        def some(i, carry):
            rows = pl.ds(i * 4, 4)
            total = work[c, rows].astype(jnp.float32) + got[c, rows].astype(jnp.float32)
            work[c, rows] = total.astype(jnp.bfloat16)
            return carry

        lax.fori_loop(0, n // 4, some, 0)

    def advance(c, stage):
        for copy in sends(c, stage):
            copy.wait_recv()
        if stage < 3:
            add(c, (got0, got1, got2)[stage], (16, 8, 4)[stage])
        else:
            total = work[c, 0].astype(jnp.float32)
            for i in range(3):
                total = total + got3[c, i].astype(jnp.float32)
            if CHUNKS[c][0]:
                work[c, 0] = total.astype(jnp.bfloat16)
            else:
                grad_ref[...] = total
        for copy in sends(c, stage + 1):
            copy.start()

    count = len(CHUNKS)
    multiply(0)
    pl.semaphore_wait(barrier, len(peers))
    swaps = [
        remote(terms.at[rep], terms.at[rep], (term_send, term_recv), i, reps[i]) for i in range(3)
    ]
    for t in range(count + LAGS[-1]):
        if t < count:
            if t:
                multiply(t)
            for copy in sends(t, 0):
                copy.start()
        if t == 0:
            for copy in swaps:
                copy.start()
        for stage, lag in enumerate(LAGS):
            if 0 <= t - lag < count:
                advance(t - lag, stage)

    for copy in swaps:
        copy.wait()
    total = terms[0].astype(jnp.float32)
    for i in range(1, 4):
        total = total + terms[i].astype(jnp.float32)
    sum_ref[...] = total

    total = grad_ref[...]
    for c in range(count):
        for copy in sends(c, 4):
            copy.wait_recv()
            total = total + got4[CHUNKS[c][0] - 1].astype(jnp.float32)
    grad_ref[...] = total
    for c in range(count):
        for stage in range(5):
            for copy in sends(c, stage):
                copy.wait_send()


def exchanged(step_count, layer_ids, inner_stack, outer_stack, activations, cotangent):
    vmem = pl.BlockSpec(memory_space=pltpu.VMEM)
    smem = pl.BlockSpec(memory_space=pltpu.SMEM)
    n = len(CHUNKS)
    block = (ROWS, COLS)
    tokens, features = activations.shape
    return pl.pallas_call(
        exchange,
        name="exchange",
        out_shape=(jax.ShapeDtypeStruct(block, jnp.float32),) * 2,
        in_specs=[smem, smem, vmem, vmem, vmem, vmem],
        out_specs=(vmem, vmem),
        scratch_shapes=[
            pltpu.VMEM((n, BLOCKS) + block, jnp.bfloat16),
            pltpu.VMEM((n, 16) + block, jnp.bfloat16),
            pltpu.VMEM((n, 8) + block, jnp.bfloat16),
            pltpu.VMEM((n, 4) + block, jnp.bfloat16),
            pltpu.VMEM((n, 3) + block, jnp.bfloat16),
            pltpu.VMEM((PLANES - 1,) + block, jnp.bfloat16),
            pltpu.VMEM((4,) + block, jnp.bfloat16),
            pltpu.SemaphoreType.DMA((n, 7)),
            pltpu.SemaphoreType.DMA((n, 7)),
            pltpu.SemaphoreType.DMA((3,)),
            pltpu.SemaphoreType.DMA((3,)),
        ],
        compiler_params=pltpu.CompilerParams(
            collective_id=0, has_side_effects=True, vmem_limit_bytes=40 * 2**20
        ),
        cost_estimate=pl.CostEstimate(
            flops=2 * tokens * features * COLS, bytes_accessed=2 * tokens * features, transcendentals=0
        ),
    )(step_count, layer_ids, inner_stack, outer_stack, activations, cotangent)


def on_device(
    inner_stack,
    outer_stack,
    outer_moment,
    layer_ids,
    step_count,
    activations,
    cotangent,
    key_weight,
    first_moment,
    second_moment,
):
    gradient, summed = exchanged(
        step_count, layer_ids, inner_stack, outer_stack, activations, cotangent
    )
    fragment = step_count[0] % FRAGS
    frag_ids = lax.dynamic_slice(layer_ids, (fragment * FRAG_LAYERS,), (FRAG_LAYERS,))
    outer_frag = jnp.take(outer_stack, frag_ids, axis=0)
    moment_frag = jnp.take(outer_moment, frag_ids, axis=0)
    outer_new, moment_new = outer_update(outer_frag, moment_frag, summed[None], 4)
    outer_out = outer_stack.at[frag_ids].set(outer_new)
    moment_out = outer_moment.at[frag_ids].set(moment_new)
    rounded = outer_new.astype(jnp.bfloat16)[None]
    inner_out = inner_stack.at[:, frag_ids].set(rounded)
    key_out, first_out, second_out = adam_update(
        key_weight, first_moment, second_moment, gradient[None], step_count
    )
    return (inner_out, outer_out, moment_out, key_out, first_out, second_out)


def solution(mesh):
    return jax.shard_map(
        on_device,
        mesh=mesh,
        in_specs=(
            P("replica", None, "fsdp", None),
            P(None, "fsdp", None),
            P(None, "fsdp", None),
            P(),
            P(),
            P(("replica", "fsdp"), None),
            P(("replica", "fsdp"), None),
            P("replica", "fsdp", None),
            P("replica", "fsdp", None),
            P("replica", "fsdp", None),
        ),
        out_specs=(
            P("replica", None, "fsdp", None),
            P(None, "fsdp", None),
            P(None, "fsdp", None),
            P("replica", "fsdp", None),
            P("replica", "fsdp", None),
            P("replica", "fsdp", None),
        ),
        check_vma=False,
    )
```

```python
import math

import jax
import jax.numpy as jnp
from jax import lax
from jax.experimental import pallas as pl
from jax.experimental.pallas import tpu as pltpu
from jax.sharding import PartitionSpec as P

BLOCK = 128
FRAGS = 4

BETA_FIRST = 0.9
BETA_SECOND = 0.95
INNER_RATE = 0.05
DECAY_RATE = 0.1
ADAM_EPSILON = 1e-08
OUTER_RATE = 0.7
OUTER_MOMENTUM = 0.9
CODE_LIMIT = 448.0
SCALE_EPSILON = 1e-06

ROWS = 16
COLS = 512
LANES = 4096
QUARTER = COLS // 4
PLANES = 8
WIDTH = 512
BLOCKS = WIDTH // ROWS
MESH = pl.DeviceIdType.MESH

CHUNKS = (3, 5, 4, 2, 6, 1, 7, 0)
QUARTERS = ("aby", "bay", "yab", "yba")
MOVES = (
    (("y", 2, 2), ("a", 0, 1), ("b", 1, 1)),
    (("b", 0, 1), ("a", 1, 2), ("b", 3, 1)),
    (("y", 0, 2), ("b", 2, 1), ("a", 3, 1)),
)
LAGS = (1, 2, 3, 4)


def exchange(
    step_hbm, ids_hbm, inner_hbm, outer_hbm, act_hbm, cot_hbm,
    grad_ref, sum_ref,
    step_ref, ids_ref, inner_ref, outer_ref, act_ref, cot_ref,
    work, got, last, terms,
    load, load_act, send, recv, term_send, term_recv, above, below,
):
    rep = lax.axis_index("replica")
    me = lax.axis_index("fsdp")
    x = lax.rem(me, 4)
    y = lax.rem(me // 4, 2)
    z = me // 8
    low = lax.rem(z, 4)
    high = z // 4
    a = lax.rem((x + 1) // 2, 2)
    b = x // 2

    def at(x_to, y_to, low_to, high_to):
        return (rep, ((high_to * 4 + low_to) * 2 + y_to) * 4 + x_to)

    along_a = at(x + 1 - 2 * lax.rem(x, 2), y, low, high)
    along_b = at(3 - x, y, low, high)
    along_y = at(x, 1 - y, low, high)
    lows = [at(x, y, lax.rem(low + i, 4), high) for i in range(1, 4)]
    highs = {d: at(x, y, low, lax.rem(high + d, PLANES)) for d in range(1, PLANES)}
    up, down = highs[1], highs[PLANES - 1]
    reps = [(lax.rem(rep + i, 4), me) for i in range(1, 4)]

    def signal(semaphore, peer):
        pl.semaphore_signal(semaphore, inc=1, device_id=peer, device_id_type=MESH)

    barrier = pltpu.get_barrier_semaphore()
    peers = [up, down, *lows, along_y, along_a, along_b, *reps]
    for peer in peers:
        signal(barrier, peer)

    count = len(CHUNKS)

    def columns(c):
        return pl.ds(pl.multiple_of(lax.rem(high + CHUNKS[c], PLANES) * WIDTH, WIDTH), WIDTH)

    def load_chunk(c):
        return pltpu.make_async_copy(
            act_hbm.at[:, columns(c)], act_ref.at[:, columns(c)], load_act.at[c]
        )

    loads = [
        pltpu.make_async_copy(src, dst, load.at[i])
        for i, (src, dst) in enumerate(
            (
                (cot_hbm, cot_ref),
                (step_hbm, step_ref),
                (ids_hbm, ids_ref),
                (inner_hbm, inner_ref),
                (outer_hbm, outer_ref),
            )
        )
    ]
    loads[0].start()
    for c in range(count):
        load_chunk(c).start()
    for copy in loads[1:]:
        copy.start()

    def remote(src, dst, sems, k, peer):
        return pltpu.make_async_remote_copy(
            src_ref=src, dst_ref=dst, send_sem=sems[0].at[k], recv_sem=sems[1].at[k],
            device_id=peer, device_id_type=MESH,
        )

    def multiply(c):
        load_chunk(c).wait()
        part = lax.dot_general(
            act_ref[:, columns(c)], cot_ref[...], (((0,), (0,)), ((), ())),
            preferred_element_type=jnp.float32,
        ).astype(jnp.bfloat16)
        for n in range(BLOCKS):
            low_to, y_to, x_to = n // 8, (n // 4) % 2, n % 4
            off_a = lax.rem(a + ((x_to + 1) // 2) % 2, 2)
            off_b = lax.rem(b + x_to // 2, 2)
            off_y = lax.rem(y + y_to, 2)
            off_m = lax.rem(low_to - low + 4, 4)
            off = {"a": off_a, "b": off_b, "y": off_y}
            for q, order in enumerate(QUARTERS):
                place = off_m
                for stage, axis in enumerate(order):
                    place = place + off[axis] * (16 >> stage)
                work[c, q, place] = part[
                    n * ROWS : (n + 1) * ROWS, q * QUARTER : (q + 1) * QUARTER
                ]

    along = {"a": along_a, "b": along_b, "y": along_y}

    def sends(c, stage):
        sems = (send.at[c], recv.at[c])
        if stage == 4:
            ahead = CHUNKS[c]
            if not ahead:
                return []
            return [remote(work.at[c, :, 0], last.at[ahead - 1], sems, 12, highs[ahead])]
        if stage == 3:
            return [
                remote(work.at[c, :, i], got.at[c, :, 27 + i], sems, 8 + i, lows[i - 1])
                for i in range(1, 4)
            ]
        held, landed = 16 >> stage, 32 - (32 >> stage)
        return [
            remote(
                work.at[c, pl.ds(q, n), pl.ds(held, held)], got.at[c, pl.ds(q, n), pl.ds(landed, held)],
                sems, 3 * stage + i, along[axis],
            )
            for i, (axis, q, n) in enumerate(MOVES[stage])
        ]

    def advance(c, stage):
        for copy in sends(c, stage):
            copy.wait_recv()
        if stage == 3:
            for q in range(4):
                total = work[c, q, 0].astype(jnp.float32)
                for i in range(28, 31):
                    total = total + got[c, q, i].astype(jnp.float32)
                if CHUNKS[c]:
                    work[c, q, 0] = total.astype(jnp.bfloat16)
                else:
                    grad_ref[:, q * QUARTER : (q + 1) * QUARTER] = total
        else:
            held, landed = 16 >> stage, 32 - (32 >> stage)

            def some(i, carry):
                mine, theirs = pl.ds(i * 4, 4), pl.ds(landed + i * 4, 4)
                for q in range(4):
                    total = work[c, q, mine].astype(jnp.float32)
                    total = total + got[c, q, theirs].astype(jnp.float32)
                    work[c, q, mine] = total.astype(jnp.bfloat16)
                return carry

            lax.fori_loop(0, held // 4, some, 0)
        for copy in sends(c, stage + 1):
            copy.start()

    loads[0].wait()
    multiply(0)
    pl.semaphore_wait(barrier, len(peers))
    signal(above.at[0], down)
    signal(below.at[0], up)
    swaps = [
        remote(terms.at[rep], terms.at[rep], (term_send, term_recv), i, reps[i]) for i in range(3)
    ]
    for t in range(count + LAGS[-1]):
        if t < count:
            if t:
                multiply(t)
            for copy in sends(t, 0):
                copy.start()
        if t == 0:
            for copy in loads[1:]:
                copy.wait()
            frag = ids_ref[lax.rem(step_ref[0], FRAGS)]
            deltas = outer_ref[frag] - inner_ref[0, frag].astype(jnp.float32)
            for k in range(COLS // BLOCK):
                part = deltas[:, k * BLOCK : (k + 1) * BLOCK]
                scale = (
                    jnp.max(jnp.abs(part), axis=-1, keepdims=True) / CODE_LIMIT + SCALE_EPSILON
                )
                coded = (part / scale).astype(jnp.bfloat16).astype(jnp.float32)
                terms[rep, :, k * BLOCK : (k + 1) * BLOCK] = (coded * scale).astype(jnp.bfloat16)
            for copy in swaps:
                copy.start()
        if 1 <= t <= 3:
            pl.semaphore_wait(above.at[t - 1], 1)
            if t < 3:
                pl.semaphore_wait(below.at[t - 1], 1)
                signal(above.at[t], down)
            if t < 2:
                signal(below.at[t], up)
        if t == count - 1:
            for copy in swaps:
                copy.wait()
            total = terms[0].astype(jnp.float32)
            for i in range(1, 4):
                total = total + terms[i].astype(jnp.float32)
            sum_ref[...] = total
        for stage, lag in enumerate(LAGS):
            if 0 <= t - lag < count:
                advance(t - lag, stage)

    for c in range(count):
        for copy in sends(c, 4):
            copy.wait_recv()
    for q in range(4):
        lanes = slice(q * QUARTER, (q + 1) * QUARTER)
        total = grad_ref[:, lanes]
        for i in range(PLANES - 1):
            total = total + last[i, q].astype(jnp.float32)
        grad_ref[:, lanes] = total
    for c in range(count):
        for stage in range(5):
            for copy in sends(c, stage):
                copy.wait_send()


def exchanged(step_count, layer_ids, inner_stack, outer_stack, activations, cotangent):
    vmem = pl.BlockSpec(memory_space=pltpu.VMEM)
    hbm = pl.BlockSpec(memory_space=pltpu.HBM)
    n = len(CHUNKS)
    block = (ROWS, QUARTER)
    tokens, features = activations.shape
    return pl.pallas_call(
        exchange,
        name="exchange",
        out_shape=(jax.ShapeDtypeStruct((ROWS, COLS), jnp.float32),) * 2,
        in_specs=[hbm] * 6,
        out_specs=(vmem, vmem),
        scratch_shapes=[
            pltpu.SMEM(step_count.shape, jnp.int32),
            pltpu.SMEM(layer_ids.shape, jnp.int32),
            pltpu.VMEM(inner_stack.shape, jnp.bfloat16),
            pltpu.VMEM(outer_stack.shape, jnp.float32),
            pltpu.VMEM(activations.shape, jnp.bfloat16),
            pltpu.VMEM(cotangent.shape, jnp.bfloat16),
            pltpu.VMEM((n, 4, BLOCKS) + block, jnp.bfloat16),
            pltpu.VMEM((n, 4, BLOCKS - 1) + block, jnp.bfloat16),
            pltpu.VMEM((PLANES - 1, 4) + block, jnp.bfloat16),
            pltpu.VMEM((4, ROWS, COLS), jnp.bfloat16),
            pltpu.SemaphoreType.DMA((5,)),
            pltpu.SemaphoreType.DMA((n,)),
            pltpu.SemaphoreType.DMA((n, 13)),
            pltpu.SemaphoreType.DMA((n, 13)),
            pltpu.SemaphoreType.DMA((3,)),
            pltpu.SemaphoreType.DMA((3,)),
            pltpu.SemaphoreType.REGULAR((3,)),
            pltpu.SemaphoreType.REGULAR((2,)),
        ],
        compiler_params=pltpu.CompilerParams(
            collective_id=0, has_side_effects=True, vmem_limit_bytes=62 * 2**20
        ),
        cost_estimate=pl.CostEstimate(
            flops=2 * tokens * features * COLS, bytes_accessed=2 * tokens * features, transcendentals=0
        ),
    )(step_count, layer_ids, inner_stack, outer_stack, activations, cotangent)


def finish(
    step_ref, ids_ref, sum_ref, grad_ref, inner_ref, outer_ref, moment_ref, key_ref, first_ref, second_ref,
    inner_out, outer_out, moment_out, key_out, first_out, second_out,
):
    frag = ids_ref[lax.rem(step_ref[0], FRAGS)]
    average = sum_ref[...] / 4
    outer_frag = outer_ref[frag]
    moment_new = OUTER_MOMENTUM * moment_ref[frag] + average
    outer_new = outer_frag - OUTER_RATE * (OUTER_MOMENTUM * moment_new + average)
    rounded = outer_new.astype(jnp.bfloat16)
    for layer in range(outer_ref.shape[0]):
        taken = frag == layer
        inner_out[0, layer] = jnp.where(taken, rounded, inner_ref[0, layer])
        outer_out[layer] = jnp.where(taken, outer_new, outer_ref[layer])
        moment_out[layer] = jnp.where(taken, moment_new, moment_ref[layer])

    gradient = grad_ref[...]
    counter = jnp.full((8, 128), step_ref[0] + 1, jnp.int32).astype(jnp.float32)
    first_left = 1.0 - jnp.exp(counter * math.log(BETA_FIRST))[:1, :1]
    second_left = 1.0 - jnp.exp(counter * math.log(BETA_SECOND))[:1, :1]
    first_new = BETA_FIRST * first_ref[0] + (1.0 - BETA_FIRST) * gradient
    second_new = BETA_SECOND * second_ref[0] + (1.0 - BETA_SECOND) * gradient * gradient
    first_hat = first_new / first_left
    second_hat = second_new / second_left
    widened = key_ref[0].astype(jnp.float32)
    moved = widened - INNER_RATE * (
        first_hat / (jnp.sqrt(second_hat) + ADAM_EPSILON) + DECAY_RATE * widened
    )
    key_out[0] = moved.astype(jnp.bfloat16)
    first_out[0] = first_new
    second_out[0] = second_new


def on_device(
    inner_stack,
    outer_stack,
    outer_moment,
    layer_ids,
    step_count,
    activations,
    cotangent,
    key_weight,
    first_moment,
    second_moment,
):
    gradient, summed = exchanged(
        step_count, layer_ids, inner_stack, outer_stack, activations, cotangent
    )
    vmem = pl.BlockSpec(memory_space=pltpu.VMEM)
    smem = pl.BlockSpec(memory_space=pltpu.SMEM)
    like = (inner_stack, outer_stack, outer_moment, key_weight, first_moment, second_moment)
    return pl.pallas_call(
        finish,
        name="finish",
        out_shape=tuple(jax.ShapeDtypeStruct(v.shape, v.dtype) for v in like),
        in_specs=[smem] * 2 + [vmem] * 8,
        out_specs=(vmem,) * 6,
    )(step_count, layer_ids, summed, gradient, *like)


def solution(mesh):
    return jax.shard_map(
        on_device,
        mesh=mesh,
        in_specs=(
            P("replica", None, "fsdp", None),
            P(None, "fsdp", None),
            P(None, "fsdp", None),
            P(),
            P(),
            P(("replica", "fsdp"), None),
            P(("replica", "fsdp"), None),
            P("replica", "fsdp", None),
            P("replica", "fsdp", None),
            P("replica", "fsdp", None),
        ),
        out_specs=(
            P("replica", None, "fsdp", None),
            P(None, "fsdp", None),
            P(None, "fsdp", None),
            P("replica", "fsdp", None),
            P("replica", "fsdp", None),
            P("replica", "fsdp", None),
        ),
        check_vma=False,
    )
```

```python
import math

import jax
import jax.numpy as jnp
from jax import lax
from jax.experimental import pallas as pl
from jax.experimental.pallas import tpu as pltpu
from jax.sharding import PartitionSpec as P

BLOCK = 128
FRAGS = 4

BETA_FIRST = 0.9
BETA_SECOND = 0.95
INNER_RATE = 0.05
DECAY_RATE = 0.1
ADAM_EPSILON = 1e-08
OUTER_RATE = 0.7
OUTER_MOMENTUM = 0.9
CODE_LIMIT = 448.0
SCALE_EPSILON = 1e-06

ROWS = 16
COLS = 512
LANES = 4096
QUARTER = COLS // 4
PLANES = 8
WIDTH = 512
BLOCKS = WIDTH // ROWS
MESH = pl.DeviceIdType.MESH

CHUNKS = (3, 5, 4, 2, 6, 1, 7, 0)
QUARTERS = ("aby", "bay", "yab", "yba")
MOVES = (
    (("y", 2, 2), ("a", 0, 1), ("b", 1, 1)),
    (("b", 0, 1), ("a", 1, 2), ("b", 3, 1)),
    (("y", 0, 2), ("b", 2, 1), ("a", 3, 1)),
)
LAGS = (1, 2, 3, 4)


def exchange(
    step_hbm, ids_hbm, inner_hbm, outer_hbm, act_hbm, cot_hbm,
    grad_ref, sum_ref,
    step_ref, ids_ref, inner_ref, outer_ref, act_ref, cot_ref,
    work, got, last, terms,
    load, load_act, send, recv, term_send, term_recv, above, below,
):
    rep = lax.axis_index("replica")
    me = lax.axis_index("fsdp")
    x = lax.rem(me, 4)
    y = lax.rem(me // 4, 2)
    z = me // 8
    low = lax.rem(z, 4)
    high = z // 4
    a = lax.rem((x + 1) // 2, 2)
    b = x // 2

    def at(x_to, y_to, low_to, high_to):
        return (rep, ((high_to * 4 + low_to) * 2 + y_to) * 4 + x_to)

    along_a = at(x + 1 - 2 * lax.rem(x, 2), y, low, high)
    along_b = at(3 - x, y, low, high)
    along_y = at(x, 1 - y, low, high)
    lows = [at(x, y, lax.rem(low + i, 4), high) for i in range(1, 4)]
    highs = {d: at(x, y, low, lax.rem(high + d, PLANES)) for d in range(1, PLANES)}
    up, down = highs[1], highs[PLANES - 1]
    reps = [(lax.rem(rep + i, 4), me) for i in range(1, 4)]

    def signal(semaphore, peer):
        pl.semaphore_signal(semaphore, inc=1, device_id=peer, device_id_type=MESH)

    barrier = pltpu.get_barrier_semaphore()
    peers = [up, down, *lows, along_y, along_a, along_b, *reps]
    for peer in peers:
        signal(barrier, peer)

    count = len(CHUNKS)

    def columns(c):
        return pl.ds(pl.multiple_of(lax.rem(high + CHUNKS[c], PLANES) * WIDTH, WIDTH), WIDTH)

    def load_chunk(c):
        return pltpu.make_async_copy(
            act_hbm.at[:, columns(c)], act_ref.at[:, columns(c)], load_act.at[c]
        )

    loads = [
        pltpu.make_async_copy(src, dst, load.at[i])
        for i, (src, dst) in enumerate(
            (
                (cot_hbm, cot_ref),
                (step_hbm, step_ref),
                (ids_hbm, ids_ref),
                (inner_hbm, inner_ref),
                (outer_hbm, outer_ref),
            )
        )
    ]
    loads[0].start()
    for c in range(count):
        load_chunk(c).start()
    for copy in loads[1:]:
        copy.start()

    def remote(src, dst, sems, k, peer):
        return pltpu.make_async_remote_copy(
            src_ref=src, dst_ref=dst, send_sem=sems[0].at[k], recv_sem=sems[1].at[k],
            device_id=peer, device_id_type=MESH,
        )

    def multiply(c):
        load_chunk(c).wait()
        part = lax.dot_general(
            act_ref[:, columns(c)], cot_ref[...], (((0,), (0,)), ((), ())),
            preferred_element_type=jnp.float32,
        ).astype(jnp.bfloat16)
        for n in range(BLOCKS):
            low_to, y_to, x_to = n // 8, (n // 4) % 2, n % 4
            off_a = lax.rem(a + ((x_to + 1) // 2) % 2, 2)
            off_b = lax.rem(b + x_to // 2, 2)
            off_y = lax.rem(y + y_to, 2)
            off_m = lax.rem(low_to - low + 4, 4)
            off = {"a": off_a, "b": off_b, "y": off_y}
            for q, order in enumerate(QUARTERS):
                place = off_m
                for stage, axis in enumerate(order):
                    place = place + off[axis] * (16 >> stage)
                work[c, q, place] = part[
                    n * ROWS : (n + 1) * ROWS, q * QUARTER : (q + 1) * QUARTER
                ]

    along = {"a": along_a, "b": along_b, "y": along_y}

    def sends(c, stage):
        sems = (send.at[c], recv.at[c])
        if stage == 4:
            ahead = CHUNKS[c]
            if not ahead:
                return []
            return [remote(work.at[c, :, 0], last.at[ahead - 1], sems, 12, highs[ahead])]
        if stage == 3:
            return [
                remote(work.at[c, :, i], got.at[c, :, 27 + i], sems, 8 + i, lows[i - 1])
                for i in range(1, 4)
            ]
        held, landed = 16 >> stage, 32 - (32 >> stage)
        return [
            remote(
                work.at[c, pl.ds(q, n), pl.ds(held, held)], got.at[c, pl.ds(q, n), pl.ds(landed, held)],
                sems, 3 * stage + i, along[axis],
            )
            for i, (axis, q, n) in enumerate(MOVES[stage])
        ]

    def advance(c, stage):
        for copy in sends(c, stage):
            copy.wait_recv()
        if stage == 3:
            for q in range(4):
                total = work[c, q, 0].astype(jnp.float32)
                for i in range(28, 31):
                    total = total + got[c, q, i].astype(jnp.float32)
                if CHUNKS[c]:
                    work[c, q, 0] = total.astype(jnp.bfloat16)
                else:
                    grad_ref[:, q * QUARTER : (q + 1) * QUARTER] = total
        else:
            held, landed = 16 >> stage, 32 - (32 >> stage)

            def some(i, carry):
                mine, theirs = pl.ds(i * 4, 4), pl.ds(landed + i * 4, 4)
                for q in range(4):
                    total = work[c, q, mine].astype(jnp.float32)
                    total = total + got[c, q, theirs].astype(jnp.float32)
                    work[c, q, mine] = total.astype(jnp.bfloat16)
                return carry

            lax.fori_loop(0, held // 4, some, 0)
        for copy in sends(c, stage + 1):
            copy.start()

    loads[0].wait()
    multiply(0)
    pl.semaphore_wait(barrier, len(peers))
    signal(above.at[0], down)
    signal(below.at[0], up)
    swaps = [
        remote(terms.at[rep], terms.at[rep], (term_send, term_recv), i, reps[i]) for i in range(3)
    ]
    for t in range(count + LAGS[-1]):
        if t < count:
            for copy in sends(t, 0):
                copy.start()
        if t + 1 < count:
            multiply(t + 1)
        if t == 2:
            for copy in loads[1:]:
                copy.wait()
            frag = ids_ref[lax.rem(step_ref[0], FRAGS)]
            deltas = outer_ref[frag] - inner_ref[0, frag].astype(jnp.float32)
            for k in range(COLS // BLOCK):
                part = deltas[:, k * BLOCK : (k + 1) * BLOCK]
                scale = (
                    jnp.max(jnp.abs(part), axis=-1, keepdims=True) / CODE_LIMIT + SCALE_EPSILON
                )
                coded = (part / scale).astype(jnp.bfloat16).astype(jnp.float32)
                terms[rep, :, k * BLOCK : (k + 1) * BLOCK] = (coded * scale).astype(jnp.bfloat16)
            for copy in swaps:
                copy.start()
        if 1 <= t <= 3:
            pl.semaphore_wait(above.at[t - 1], 1)
            if t < 3:
                pl.semaphore_wait(below.at[t - 1], 1)
                signal(above.at[t], down)
            if t < 2:
                signal(below.at[t], up)
        if t == count - 1:
            for copy in swaps:
                copy.wait()
            total = terms[0].astype(jnp.float32)
            for i in range(1, 4):
                total = total + terms[i].astype(jnp.float32)
            sum_ref[...] = total
        for stage, lag in enumerate(LAGS):
            if 0 <= t - lag < count:
                advance(t - lag, stage)

    for c in range(count):
        for copy in sends(c, 4):
            copy.wait_recv()
    for q in range(4):
        lanes = slice(q * QUARTER, (q + 1) * QUARTER)
        total = grad_ref[:, lanes]
        for i in range(PLANES - 1):
            total = total + last[i, q].astype(jnp.float32)
        grad_ref[:, lanes] = total
    for c in range(count):
        for stage in range(5):
            for copy in sends(c, stage):
                copy.wait_send()


def exchanged(step_count, layer_ids, inner_stack, outer_stack, activations, cotangent):
    vmem = pl.BlockSpec(memory_space=pltpu.VMEM)
    hbm = pl.BlockSpec(memory_space=pltpu.HBM)
    n = len(CHUNKS)
    block = (ROWS, QUARTER)
    tokens, features = activations.shape
    return pl.pallas_call(
        exchange,
        name="exchange",
        out_shape=(jax.ShapeDtypeStruct((ROWS, COLS), jnp.float32),) * 2,
        in_specs=[hbm] * 6,
        out_specs=(vmem, vmem),
        scratch_shapes=[
            pltpu.SMEM(step_count.shape, jnp.int32),
            pltpu.SMEM(layer_ids.shape, jnp.int32),
            pltpu.VMEM(inner_stack.shape, jnp.bfloat16),
            pltpu.VMEM(outer_stack.shape, jnp.float32),
            pltpu.VMEM(activations.shape, jnp.bfloat16),
            pltpu.VMEM(cotangent.shape, jnp.bfloat16),
            pltpu.VMEM((n, 4, BLOCKS) + block, jnp.bfloat16),
            pltpu.VMEM((n, 4, BLOCKS - 1) + block, jnp.bfloat16),
            pltpu.VMEM((PLANES - 1, 4) + block, jnp.bfloat16),
            pltpu.VMEM((4, ROWS, COLS), jnp.bfloat16),
            pltpu.SemaphoreType.DMA((5,)),
            pltpu.SemaphoreType.DMA((n,)),
            pltpu.SemaphoreType.DMA((n, 13)),
            pltpu.SemaphoreType.DMA((n, 13)),
            pltpu.SemaphoreType.DMA((3,)),
            pltpu.SemaphoreType.DMA((3,)),
            pltpu.SemaphoreType.REGULAR((3,)),
            pltpu.SemaphoreType.REGULAR((2,)),
        ],
        compiler_params=pltpu.CompilerParams(
            collective_id=0, has_side_effects=True, vmem_limit_bytes=62 * 2**20
        ),
        cost_estimate=pl.CostEstimate(
            flops=2 * tokens * features * COLS, bytes_accessed=2 * tokens * features, transcendentals=0
        ),
    )(step_count, layer_ids, inner_stack, outer_stack, activations, cotangent)


def finish(
    step_ref, ids_ref, sum_ref, grad_ref, inner_ref, outer_ref, moment_ref, key_ref, first_ref, second_ref,
    inner_out, outer_out, moment_out, key_out, first_out, second_out,
):
    frag = ids_ref[lax.rem(step_ref[0], FRAGS)]
    average = sum_ref[...] / 4
    outer_frag = outer_ref[frag]
    moment_new = OUTER_MOMENTUM * moment_ref[frag] + average
    outer_new = outer_frag - OUTER_RATE * (OUTER_MOMENTUM * moment_new + average)
    rounded = outer_new.astype(jnp.bfloat16)
    for layer in range(outer_ref.shape[0]):
        taken = frag == layer
        inner_out[0, layer] = jnp.where(taken, rounded, inner_ref[0, layer])
        outer_out[layer] = jnp.where(taken, outer_new, outer_ref[layer])
        moment_out[layer] = jnp.where(taken, moment_new, moment_ref[layer])

    gradient = grad_ref[...]
    counter = jnp.full((8, 128), step_ref[0] + 1, jnp.int32).astype(jnp.float32)
    first_left = 1.0 - jnp.exp(counter * math.log(BETA_FIRST))[:1, :1]
    second_left = 1.0 - jnp.exp(counter * math.log(BETA_SECOND))[:1, :1]
    first_new = BETA_FIRST * first_ref[0] + (1.0 - BETA_FIRST) * gradient
    second_new = BETA_SECOND * second_ref[0] + (1.0 - BETA_SECOND) * gradient * gradient
    first_hat = first_new / first_left
    second_hat = second_new / second_left
    widened = key_ref[0].astype(jnp.float32)
    moved = widened - INNER_RATE * (
        first_hat / (jnp.sqrt(second_hat) + ADAM_EPSILON) + DECAY_RATE * widened
    )
    key_out[0] = moved.astype(jnp.bfloat16)
    first_out[0] = first_new
    second_out[0] = second_new


def on_device(
    inner_stack,
    outer_stack,
    outer_moment,
    layer_ids,
    step_count,
    activations,
    cotangent,
    key_weight,
    first_moment,
    second_moment,
):
    gradient, summed = exchanged(
        step_count, layer_ids, inner_stack, outer_stack, activations, cotangent
    )
    vmem = pl.BlockSpec(memory_space=pltpu.VMEM)
    smem = pl.BlockSpec(memory_space=pltpu.SMEM)
    like = (inner_stack, outer_stack, outer_moment, key_weight, first_moment, second_moment)
    return pl.pallas_call(
        finish,
        name="finish",
        out_shape=tuple(jax.ShapeDtypeStruct(v.shape, v.dtype) for v in like),
        in_specs=[smem] * 2 + [vmem] * 8,
        out_specs=(vmem,) * 6,
    )(step_count, layer_ids, summed, gradient, *like)


def solution(mesh):
    return jax.shard_map(
        on_device,
        mesh=mesh,
        in_specs=(
            P("replica", None, "fsdp", None),
            P(None, "fsdp", None),
            P(None, "fsdp", None),
            P(),
            P(),
            P(("replica", "fsdp"), None),
            P(("replica", "fsdp"), None),
            P("replica", "fsdp", None),
            P("replica", "fsdp", None),
            P("replica", "fsdp", None),
        ),
        out_specs=(
            P("replica", None, "fsdp", None),
            P(None, "fsdp", None),
            P(None, "fsdp", None),
            P("replica", "fsdp", None),
            P("replica", "fsdp", None),
            P("replica", "fsdp", None),
        ),
        check_vma=False,
    )
```
